32 devices in a mesh: xy: 8 (over y, x, core), gz: 4 (over z).
Axes of the slice: x: 2, y: 2, z: 4, core: 2. Of those that a mesh axis runs over, the one named last changes fastest.
Arguments:
- volume: float32 [384, 8192], P('gz', 'xy'), may hold values from 0 to 1
- sinogram: float32 [384, 2048], P('gz', 'xy'), may hold values from 100 to 2000
- ray_mats: bfloat16 [8, 4, 256, 256], P('xy'), may hold values from 0.049804688 to 1
- offsets: int32 [8, 4], P('xy'), may hold values from 0 to 768
- ray_lists: int32 [8, 4], replicated, may hold values from 0 to 7, all different within a row
- owner_map: int32 [8], replicated, may hold values from 0 to 7, each once
Outputs:
- new_volume: float32 [384, 8192], P('gz', 'xy')
- weighted: float32 [384, 2048], P('gz', 'xy')
The draws below stay inside these ranges and needn't reach their ends.
Inputs may be any that keep to these rules, and one draw needn't show every extreme that they name: `ray_lists`: the 4 entries of a row are distinct, and every ray block is named by some row. `owner_map`: each owner appears once.
All inputs are finite; a program needn't handle non-finite values.
Results may differ from the reference program's by a relative error of at most 0.0003.
Values sent between devices are 32-bit elements; how exact they have to be, the bound alone decides.
A program may use at most 64 MiB of HBM per device.

```python
import jax
import jax.numpy as jnp
from jax import lax

VXY = 1024
W = 256
RB = 256
K = 4
NZ = 384
VOX = 8192
BLOCKS = 8


def set_ends(drawn, rng, low, top_value):
    index_at = [jax.random.randint(jax.random.fold_in(rng, axis), (), 0, length) for axis, length in enumerate(drawn.shape)]
    widest = drawn.shape.index(max(drawn.shape))
    next_to = index_at[:widest] + [(index_at[widest] + 1) % drawn.shape[widest]] + index_at[widest + 1:]
    return drawn.at[tuple(index_at)].set(low).at[tuple(next_to)].set(top_value)


def block_scale(rng, extent, pieces, smallest, top_value):
    gain = 1.0
    for dim, shards_of in pieces:
        steps = jax.random.uniform(jax.random.fold_in(jax.random.fold_in(rng, 6), dim), (shards_of,), jnp.float32, smallest / len(pieces), top_value / len(pieces))
        gain = gain * jnp.repeat(jnp.exp(steps), extent[dim] // shards_of).reshape((-1,) + (1,) * (len(extent) - 1 - dim))
    return gain


def different_ones(key, rows, count, top, lift):
    sequence = jax.random.permutation(jax.random.fold_in(key, 1), count)
    pull = sequence
    for power in range(3):
        pull = pull * pull // count
    pull = pull * lift // count
    tickets = jax.random.randint(jax.random.fold_in(key, 2), (rows, count), 0, 4096) + pull
    sure = jax.random.permutation(jax.random.fold_in(key, 3), rows)[jnp.arange(count) % rows]
    tickets = jnp.where(jnp.arange(rows)[:, None] == sure[None, :], 1 << 14, tickets)
    merit = tickets * count + jnp.arange(count)
    return lax.top_k(merit.astype(jnp.int32), top)[1].astype(jnp.int32)


def setup_inputs(seed: int = 0) -> dict:
    key_list = jax.random.split(jax.random.key(seed), 7)
    volume = jnp.clip(1.0 * jax.random.uniform(key_list[0], (NZ, VOX), jnp.float32) ** block_scale(key_list[0], (NZ, VOX), ((0, 4), (1, 8)), -0.2, 0.2), 0.0, 1.0)
    sinogram = jnp.clip(100.0 + 1900.0 * jax.random.uniform(key_list[1], (NZ, BLOCKS * RB), jnp.float32) ** block_scale(key_list[1], (NZ, BLOCKS * RB), ((0, 4), (1, 8)), -0.2, 0.2), 100.0, 2000.0)
    ray_mats = jnp.clip(0.049804688 + 0.9501953 * jax.random.uniform(key_list[2], (BLOCKS, K, W, RB), jnp.float32) ** block_scale(key_list[2], (BLOCKS, K, W, RB), ((0, 8),), -0.2, 0.2), 0.049804688, 1.0).astype(jnp.bfloat16)
    offsets = set_ends(jax.random.randint(key_list[3], (BLOCKS, K), 0, VXY - W + 1), jax.random.fold_in(key_list[3], 1), 0, VXY - W).astype(jnp.int32)
    ray_lists = different_ones(key_list[4], BLOCKS, BLOCKS, K, 4096)
    owner_map = jax.random.permutation(key_list[5], BLOCKS).astype(jnp.int32)
    return dict(volume=volume, sinogram=sinogram, ray_mats=ray_mats, offsets=offsets, ray_lists=ray_lists, owner_map=owner_map)


relax = 1.0
tv_weight = 0.2
smooth_sq = 0.01

def cut_windows(field, starts, width):
    return jax.vmap(lambda start: lax.dynamic_slice_in_dim(field, start, width, 1))(starts)

def spread_back(smeared, column_terms, starts, vxy):
    depth = smeared.shape[1]
    width = smeared.shape[2]

    def add_one(index, carry):
        update, column = carry
        start = starts[index]
        piece = lax.dynamic_slice_in_dim(update, start, width, 1) + smeared[index]
        update = lax.dynamic_update_slice_in_dim(update, piece, start, 1)
        col_piece = lax.dynamic_slice_in_dim(column, start, width, 0) + column_terms[index]
        column = lax.dynamic_update_slice_in_dim(column, col_piece, start, 0)
        return (update, column)
    init = (jnp.zeros((depth, vxy), jnp.float32), jnp.zeros((vxy,), jnp.float32))
    return lax.fori_loop(0, smeared.shape[0], add_one, init)

def total_variation(padded):
    diffs = padded[1:] - padded[:-1]
    slopes = diffs / jnp.sqrt(diffs * diffs + smooth_sq)
    return slopes[:-1] - slopes[1:]

def reference(volume, sinogram, ray_mats, offsets, ray_lists, owner_map):
    nblk = ray_mats.shape[0]
    width = ray_mats.shape[2]
    rays = ray_mats.shape[3]
    depth = volume.shape[0]
    vxy = volume.shape[1] // nblk
    blocks = volume.reshape(depth, nblk, vxy).transpose(1, 0, 2)
    owners = owner_map[ray_lists]
    order = jnp.arange(nblk, dtype=jnp.int32)

    def project(carry, block_index):
        proj, rowsum = carry
        block = blocks[block_index]
        matrix = ray_mats[block_index].astype(jnp.float32)
        windows = cut_windows(block, offsets[block_index], width)
        partial_value = jnp.einsum('kzw,kwr->kzr', windows, matrix, precision=lax.Precision.HIGHEST)
        proj = proj.at[owners[block_index]].add(partial_value)
        rowsum = rowsum.at[owners[block_index]].add(lax.optimization_barrier(jnp.sum(matrix, axis=1)))
        return ((proj, rowsum), None)
    init = (jnp.zeros((nblk, depth, rays), jnp.float32), jnp.zeros((nblk, rays), jnp.float32))
    (proj, rowsum), _ = lax.scan(project, init, order)
    measured = sinogram.reshape(depth, nblk, rays).transpose(1, 0, 2)
    weighted = (measured - proj) / rowsum[:, None, :]

    def backproject(block_index):
        matrix = ray_mats[block_index].astype(jnp.float32)
        needed = weighted[owners[block_index]]
        smeared = jnp.einsum('kzr,kwr->kzw', needed, matrix, precision=lax.Precision.HIGHEST)
        update, column = spread_back(smeared, lax.optimization_barrier(jnp.sum(matrix, axis=2)), offsets[block_index], vxy)
        return update / jnp.maximum(column, 1.0)[None, :]
    updates = lax.map(backproject, order)
    update = updates.transpose(1, 0, 2).reshape(depth, nblk * vxy)
    padded = jnp.pad(volume, ((1, 1), (0, 0)))
    new_volume = volume + relax * update - tv_weight * total_variation(padded)
    weighted_out = weighted.transpose(1, 0, 2).reshape(depth, nblk * rays)
    return (new_volume, weighted_out)
```

```python
import functools

import jax
import jax.numpy as jnp
from jax import lax
from jax.experimental import pallas as pl
from jax.experimental.pallas import tpu as pltpu
from jax.sharding import PartitionSpec as P

relax = 1.0
tv_weight = 0.2
smooth_sq = 0.01

LANES = 128
TILE = 8
CHUNKS = 2
TERMS = 3


def bit_orders(bits, chunks):
    rest = list(range(1, bits))
    return [[0] + (rest if chunk % 2 == 0 else rest[::-1]) for chunk in range(chunks)]


def split_terms(x, terms):
    parts = []
    for _ in range(terms):
        part = x.astype(jnp.bfloat16)
        parts.append(part)
        x = x - part.astype(jnp.float32)
    return parts


def flip(index, bit):
    step = 1 << bit
    return index + step * (1 - 2 * ((index // step) % 2))


def sum_slabs(stacked, terms, rows):
    total = stacked[(terms - 1) * rows : terms * rows]
    for term in range(terms - 2, -1, -1):
        total = total + stacked[term * rows : (term + 1) * rows]
    return total


def rel_of(order, position):
    bits = len(order)
    return sum(((position >> (bits - 1 - j)) & 1) << bit for j, bit in enumerate(order))


def position_of(order, owner, me):
    bits = len(order)
    place = jnp.int32(0)
    for j, bit in enumerate(order):
        step = 1 << bit
        place = place + ((owner // step + me // step) % 2) * (1 << (bits - 1 - j))
    return place


def band(offsets, k, vxy, width):
    last_base = (vxy - width) // LANES - 1
    base = jnp.minimum(offsets[0, k] // LANES, last_base)
    return base * LANES, offsets[0, k] - base * LANES


def project_kernel(cfg, vol, mats, offsets, ray_lists, owner_map, *refs):
    count, bits, depth, vxy, width, rays, listed, chunks, gz_count = cfg
    rows = depth // chunks
    orders = bit_orders(bits, chunks)
    parts = refs[:chunks]
    found = refs[chunks]
    me = lax.axis_index("xy")
    span = width + LANES
    owners = [owner_map[ray_lists[me, k]] for k in range(listed)]
    ones = jnp.ones((16, width), jnp.bfloat16)
    found[listed] = jnp.zeros((depth + TILE, rays), jnp.float32)
    for k in range(listed):
        start, shift = band(offsets, k, vxy, width)
        window = vol[:, pl.ds(pl.multiple_of(start, LANES), span)]
        window = pltpu.roll(window, span - shift, 1)[:, :width]
        lhs = jnp.concatenate(split_terms(window, TERMS) + [ones], axis=0)
        product = jnp.dot(lhs, mats[0, k], preferred_element_type=jnp.float32)
        found[k, :depth] = sum_slabs(product, TERMS, depth)
        found[k, depth:] = product[TERMS * depth : TERMS * depth + TILE]
    for position in range(count):
        for chunk in range(chunks):
            rel = rel_of(orders[chunk], position)
            owner = me
            for bit in range(bits):
                if (rel >> bit) & 1:
                    owner = flip(owner, bit)
            slot = jnp.int32(listed)
            for k in range(listed):
                slot = jnp.where(owners[k] == owner, jnp.int32(k), slot)
            top = chunk * rows
            parts[chunk][position, :rows] = found[slot, top : top + rows]
            if chunk == 0:
                parts[chunk][position, rows:] = found[slot, depth:]


def exchange_kernel(cfg, vol, sino, mats, *refs):
    count, bits, depth, vxy, width, rays, listed, chunks, gz_count = cfg
    rows = depth // chunks
    half = count // 2
    orders = bit_orders(bits, chunks)
    refs = list(refs)

    def take(number):
        taken = refs[:number]
        del refs[:number]
        return taken

    parts = take(chunks)
    ray_values = take(chunks)
    terms, smoothed = take(2)
    sums = take(chunks)
    landed = take(chunks)
    padded, send_sem, recv_sem, halo_send, halo_recv = refs

    me = lax.axis_index("xy")
    slab = lax.axis_index("gz")
    partners = [flip(me, bit) for bit in range(bits)]

    barrier = pltpu.get_barrier_semaphore()
    for partner in partners:
        pl.semaphore_signal(barrier, inc=1, device_id={"xy": partner}, device_id_type=pl.DeviceIdType.MESH)

    @pl.when(slab > 0)
    def _():
        pl.semaphore_signal(barrier, inc=1, device_id={"gz": slab - 1}, device_id_type=pl.DeviceIdType.MESH)

    @pl.when(slab < gz_count - 1)
    def _():
        pl.semaphore_signal(barrier, inc=1, device_id={"gz": slab + 1}, device_id_type=pl.DeviceIdType.MESH)

    has_below = (slab > 0).astype(jnp.int32)
    has_above = (slab < gz_count - 1).astype(jnp.int32)
    pl.semaphore_wait(barrier, bits + has_below + has_above)

    def remote(src, dst, chunk, number, partner):
        return pltpu.make_async_remote_copy(
            src_ref=src,
            dst_ref=dst,
            send_sem=send_sem.at[chunk, number],
            recv_sem=recv_sem.at[chunk, number],
            device_id={"xy": partner},
            device_id_type=pl.DeviceIdType.MESH,
        )

    pending = []
    live = {}

    def reduce_send(chunk, stage):
        low = half >> stage
        source = parts[chunk] if stage == 0 else sums[chunk]
        copy = remote(
            source.at[pl.ds(low, low)],
            landed[chunk].at[pl.ds(low, low)],
            chunk,
            stage,
            partners[orders[chunk][stage]],
        )
        copy.start()
        live[chunk] = copy
        pending.append(copy)

    def add_landed(chunk, stage, positions):
        low = half >> stage
        source = parts[chunk] if stage == 0 else sums[chunk]
        for position in positions:
            sums[chunk][position] = source[position] + landed[chunk][low + position]

    def gather_send(chunk, stage):
        held = count >> (stage + 1)
        copy = remote(
            ray_values[chunk].at[pl.ds(0, held)],
            ray_values[chunk].at[pl.ds(held, held)],
            chunk,
            bits + stage,
            partners[orders[chunk][stage]],
        )
        copy.start()
        live[chunk] = copy
        pending.append(copy)

    def halo_up():
        return pltpu.make_async_remote_copy(
            src_ref=vol.at[pl.ds(depth - TILE, TILE)],
            dst_ref=padded.at[pl.ds(0, TILE)],
            send_sem=halo_send.at[0],
            recv_sem=halo_recv.at[0],
            device_id={"gz": slab + 1},
            device_id_type=pl.DeviceIdType.MESH,
        )

    def halo_down():
        return pltpu.make_async_remote_copy(
            src_ref=vol.at[pl.ds(0, TILE)],
            dst_ref=padded.at[pl.ds(TILE + depth, TILE)],
            send_sem=halo_send.at[1],
            recv_sem=halo_recv.at[1],
            device_id={"gz": slab - 1},
            device_id_type=pl.DeviceIdType.MESH,
        )

    for chunk in range(chunks):
        reduce_send(chunk, 0)

    @pl.when(slab < gz_count - 1)
    def _():
        halo_up().start()

    @pl.when(slab > 0)
    def _():
        halo_down().start()

    for stage in range(1, bits):
        for chunk in range(chunks):
            live[chunk].wait_recv()
            low = half >> stage
            add_landed(chunk, stage - 1, range(low, 2 * low))
            reduce_send(chunk, stage)
            add_landed(chunk, stage - 1, range(low))

        if stage == 1:
            ones = jnp.ones((16, rays), jnp.bfloat16)
            for k in range(listed):
                terms[k] = lax.dot_general(
                    ones, mats[0, k], (((1,), (1,)), ((), ())), preferred_element_type=jnp.float32
                )[:TILE]
            padded[TILE : TILE + depth, :] = vol[...]

            @pl.when(slab == 0)
            def _():
                padded[:TILE, :] = jnp.zeros((TILE, vxy), jnp.float32)

            @pl.when(slab == gz_count - 1)
            def _():
                padded[TILE + depth :, :] = jnp.zeros((TILE, vxy), jnp.float32)

    def smooth():
        @pl.when(slab > 0)
        def _():
            halo_up().wait_recv()

        @pl.when(slab < gz_count - 1)
        def _():
            halo_down().wait_recv()

        for lane in range(0, vxy, LANES):
            lanes = slice(lane, lane + LANES)
            diffs = padded[TILE : TILE + depth + 1, lanes] - padded[TILE - 1 : TILE + depth, lanes]
            slopes = diffs * lax.rsqrt(diffs * diffs + smooth_sq)
            smoothed[:, lanes] = vol[:, lanes] - tv_weight * (slopes[:depth] - slopes[1:])

    smooth()
    rowsum = None
    for chunk in range(chunks):
        live[chunk].wait_recv()
        add_landed(chunk, bits - 1, [0])
        total = sums[chunk][0]
        if chunk == 0:
            rowsum = total[rows : rows + 1]
        top = chunk * rows
        ray_values[chunk][0] = (sino[top : top + rows, :] - total[:rows]) / rowsum
        gather_send(chunk, bits - 1)
    for stage in range(bits - 2, -1, -1):
        for chunk in range(chunks):
            live[chunk].wait_recv()
            gather_send(chunk, stage)
    for chunk in range(chunks):
        live[chunk].wait_recv()
    for copy in pending:
        copy.wait_send()

    @pl.when(slab < gz_count - 1)
    def _():
        halo_up().wait_send()

    @pl.when(slab > 0)
    def _():
        halo_down().wait_send()


def back_kernel(cfg, smoothed, terms, mats, offsets, ray_lists, owner_map, *refs):
    count, bits, depth, vxy, width, rays, listed, chunks, gz_count = cfg
    rows = depth // chunks
    orders = bit_orders(bits, chunks)
    ray_values = refs[:chunks]
    new_vol, weighted_out, spread = refs[chunks:]
    me = lax.axis_index("xy")
    span = width + LANES
    margin = vxy - span
    high = depth + TILE
    for chunk in range(chunks):
        weighted_out[chunk * rows : (chunk + 1) * rows, :] = ray_values[chunk][0]
    spread[:, :, :margin] = jnp.zeros((listed, high, margin), jnp.float32)
    spread[:, :, margin + span :] = jnp.zeros((listed, high, margin), jnp.float32)
    places = []
    for k in range(listed):
        owner = owner_map[ray_lists[me, k]]
        needed = jnp.concatenate(
            [ray_values[c][position_of(orders[c], owner, me)] for c in range(chunks)], axis=0
        )
        stacked = lax.dot_general(
            jnp.concatenate(split_terms(needed, TERMS), axis=0),
            mats[0, k],
            (((1,), (1,)), ((), ())),
            preferred_element_type=jnp.float32,
        )
        start, shift = band(offsets, k, vxy, width)
        piece = jnp.concatenate([sum_slabs(stacked, TERMS, depth), terms[k]], axis=0)
        wide = jnp.concatenate([piece, jnp.zeros((high, LANES), jnp.float32)], axis=1)
        spread[k, :, margin : margin + span] = pltpu.roll(wide, shift, 1)
        places.append(margin - start)
    for lane in range(0, vxy, LANES):
        total = None
        for k in range(listed):
            piece = spread[k, :, pl.ds(pl.multiple_of(places[k] + lane, LANES), LANES)]
            total = piece if total is None else total + piece
        lanes = slice(lane, lane + LANES)
        scale = relax / jnp.maximum(total[depth : depth + 1], 1.0)
        new_vol[:, lanes] = smoothed[:, lanes] + total[:depth] * scale


def per_device(cfg, volume, sinogram, ray_mats, offsets, ray_lists, owner_map):
    count, bits, depth, vxy, width, rays, listed, chunks, gz_count = cfg
    rows = depth // chunks
    high = [rows + (TILE if chunk == 0 else 0) for chunk in range(chunks)]
    f32 = jnp.float32
    vmem = pl.BlockSpec(memory_space=pltpu.VMEM)
    smem = pl.BlockSpec(memory_space=pltpu.SMEM)
    limit = 24 * 1024 * 1024

    def shape(*dims):
        return jax.ShapeDtypeStruct(dims, f32)

    parts = pl.pallas_call(
        functools.partial(project_kernel, cfg),
        out_shape=tuple(shape(count, h, rays) for h in high),
        in_specs=[vmem, vmem, smem, smem, smem],
        out_specs=(vmem,) * chunks,
        scratch_shapes=[pltpu.VMEM((listed + 1, depth + TILE, rays), f32)],
        compiler_params=pltpu.CompilerParams(vmem_limit_bytes=limit),
    )(volume, ray_mats, offsets, ray_lists, owner_map)

    *ray_values, terms, smoothed = pl.pallas_call(
        functools.partial(exchange_kernel, cfg),
        out_shape=tuple(shape(count, rows, rays) for _ in range(chunks))
        + (shape(listed, TILE, width), shape(depth, vxy)),
        in_specs=[vmem] * (3 + chunks),
        out_specs=(vmem,) * (chunks + 2),
        scratch_shapes=[pltpu.VMEM((count // 2, h, rays), f32) for h in high]
        + [pltpu.VMEM((count, h, rays), f32) for h in high]
        + [
            pltpu.VMEM((depth + 2 * TILE, vxy), f32),
            pltpu.SemaphoreType.DMA((chunks, 2 * bits)),
            pltpu.SemaphoreType.DMA((chunks, 2 * bits)),
            pltpu.SemaphoreType.DMA((2,)),
            pltpu.SemaphoreType.DMA((2,)),
        ],
        compiler_params=pltpu.CompilerParams(
            collective_id=0, has_side_effects=True, vmem_limit_bytes=limit
        ),
    )(volume, sinogram, ray_mats, *parts)

    return pl.pallas_call(
        functools.partial(back_kernel, cfg),
        out_shape=(shape(depth, vxy), shape(depth, rays)),
        in_specs=[vmem] * 3 + [smem] * 3 + [vmem] * chunks,
        out_specs=(vmem, vmem),
        scratch_shapes=[pltpu.VMEM((listed, depth + TILE, 2 * vxy - width - LANES), f32)],
        compiler_params=pltpu.CompilerParams(vmem_limit_bytes=limit),
    )(smoothed, terms, ray_mats, offsets, ray_lists, owner_map, *ray_values)


def solution(mesh):
    in_specs = (P("gz", "xy"), P("gz", "xy"), P("xy", None, None, None), P("xy", None), P(), P())
    out_specs = (P("gz", "xy"), P("gz", "xy"))
    count = mesh.shape["xy"]
    gz_count = mesh.shape["gz"]

    def whole(volume, sinogram, ray_mats, offsets, ray_lists, owner_map):
        cfg = (
            count,
            count.bit_length() - 1,
            volume.shape[0] // gz_count,
            volume.shape[1] // count,
            ray_mats.shape[2],
            ray_mats.shape[3],
            ray_mats.shape[1],
            CHUNKS,
            gz_count,
        )
        return jax.shard_map(
            functools.partial(per_device, cfg),
            mesh=mesh,
            in_specs=in_specs,
            out_specs=out_specs,
            check_vma=False,
        )(volume, sinogram, ray_mats, offsets, ray_lists, owner_map)

    return whole
```

```python
import functools

import jax
import jax.numpy as jnp
from jax import lax
from jax.experimental import pallas as pl
from jax.experimental.pallas import tpu as pltpu
from jax.sharding import PartitionSpec as P

relax = 1.0
tv_weight = 0.2
smooth_sq = 0.01

LANES = 128
TILE = 8
CHUNKS = 3
TERMS = 3


def split_terms(x, terms):
    parts = []
    for _ in range(terms):
        part = x.astype(jnp.bfloat16)
        parts.append(part)
        x = x - part.astype(jnp.float32)
    return parts


def flip(index, bit):
    step = 1 << bit
    return index + step * (1 - 2 * ((index // step) % 2))


def sum_slabs(stacked, terms, rows):
    total = stacked[(terms - 1) * rows : terms * rows]
    for term in range(terms - 2, -1, -1):
        total = total + stacked[term * rows : (term + 1) * rows]
    return total


def partner_at(me, position, bits):
    other = flip(me, 0) if (position >> (bits - 1)) & 1 else me
    for bit in range(1, bits):
        if (position >> (bit - 1)) & 1:
            other = flip(other, bit)
    return other


def position_of(owner, me, bits):
    place = ((owner + me) % 2) * (1 << (bits - 1))
    for bit in range(1, bits):
        step = 1 << bit
        place = place + ((owner // step + me // step) % 2) * (1 << (bit - 1))
    return place


def band(offsets, k, vxy, width):
    last_base = (vxy - width) // LANES - 1
    base = jnp.minimum(offsets[0, k] // LANES, last_base)
    return base * LANES, offsets[0, k] - base * LANES


def project_kernel(cfg, vol, mats, offsets, lists, owner_map, *refs):
    count, bits, depth, vxy, width, rays, listed, chunks, gz_count = cfg
    rows = depth // chunks
    parts = refs[:chunks]
    found = refs[chunks]
    me = lax.axis_index("xy")
    span = width + LANES
    owners = [owner_map[lists[k, me]] for k in range(listed)]
    ones = jnp.ones((16, width), jnp.bfloat16)
    found[listed] = jnp.zeros((depth + TILE, rays), jnp.float32)
    for k in range(listed):
        start, shift = band(offsets, k, vxy, width)
        window = vol[:, pl.ds(pl.multiple_of(start, LANES), span)]
        window = pltpu.roll(window, span - shift, 1)[:, :width]
        lhs = jnp.concatenate(split_terms(window, TERMS) + [ones], axis=0)
        product = jnp.dot(lhs, mats[0, k], preferred_element_type=jnp.float32)
        found[k, :depth] = sum_slabs(product, TERMS, depth)
        found[k, depth:] = product[TERMS * depth : TERMS * depth + TILE]
    for position in range(count):
        owner = partner_at(me, position, bits)
        slot = jnp.int32(listed)
        for k in range(listed):
            slot = jnp.where(owners[k] == owner, jnp.int32(k), slot)
        for chunk in range(chunks):
            top = chunk * rows
            parts[chunk][position, :rows] = found[slot, top : top + rows]
            if chunk == 0:
                parts[chunk][position, rows:] = found[slot, depth:]


def exchange_kernel(cfg, vol, sino, mats, *refs):
    count, bits, depth, vxy, width, rays, listed, chunks, gz_count = cfg
    rows = depth // chunks
    half = count // 2
    refs = list(refs)

    def take(number):
        taken = refs[:number]
        del refs[:number]
        return taken

    parts = take(chunks)
    ray_values = take(chunks)
    terms, smoothed = take(2)
    sums = take(chunks)
    landed = take(chunks)
    padded, send_sem, recv_sem, halo_send, halo_recv = refs

    me = lax.axis_index("xy")
    slab = lax.axis_index("gz")
    sibling = flip(me, 0)
    direct = list(range(half - 1, 0, -1))
    partners = [sibling] + [partner_at(me, p, bits) for p in range(1, half)]

    barrier = pltpu.get_barrier_semaphore()
    for partner in partners:
        pl.semaphore_signal(barrier, inc=1, device_id={"xy": partner}, device_id_type=pl.DeviceIdType.MESH)

    @pl.when(slab > 0)
    def _():
        pl.semaphore_signal(barrier, inc=1, device_id={"gz": slab - 1}, device_id_type=pl.DeviceIdType.MESH)

    @pl.when(slab < gz_count - 1)
    def _():
        pl.semaphore_signal(barrier, inc=1, device_id={"gz": slab + 1}, device_id_type=pl.DeviceIdType.MESH)

    has_below = (slab > 0).astype(jnp.int32)
    has_above = (slab < gz_count - 1).astype(jnp.int32)
    pl.semaphore_wait(barrier, half + has_below + has_above)

    def remote(src, dst, chunk, number, partner):
        return pltpu.make_async_remote_copy(
            src_ref=src,
            dst_ref=dst,
            send_sem=send_sem.at[chunk, number],
            recv_sem=recv_sem.at[chunk, number],
            device_id={"xy": partner},
            device_id_type=pl.DeviceIdType.MESH,
        )

    def sibling_parts(chunk):
        return remote(
            parts[chunk].at[pl.ds(half, half)], landed[chunk].at[pl.ds(half, half)], chunk, 0, sibling
        )

    def reduce_copy(chunk, p):
        return remote(sums[chunk].at[p], landed[chunk].at[p], chunk, p, partners[p])

    def gather_copy(chunk, p):
        return remote(ray_values[chunk].at[0], ray_values[chunk].at[p], chunk, half + p, partners[p])

    def relay_copy(chunk, p):
        return remote(
            ray_values[chunk].at[p], ray_values[chunk].at[half + p], chunk, 2 * half + p, sibling
        )

    def halo_up():
        return pltpu.make_async_remote_copy(
            src_ref=vol.at[pl.ds(depth - TILE, TILE)],
            dst_ref=padded.at[pl.ds(0, TILE)],
            send_sem=halo_send.at[0],
            recv_sem=halo_recv.at[0],
            device_id={"gz": slab + 1},
            device_id_type=pl.DeviceIdType.MESH,
        )

    def halo_down():
        return pltpu.make_async_remote_copy(
            src_ref=vol.at[pl.ds(0, TILE)],
            dst_ref=padded.at[pl.ds(TILE + depth, TILE)],
            send_sem=halo_send.at[1],
            recv_sem=halo_recv.at[1],
            device_id={"gz": slab - 1},
            device_id_type=pl.DeviceIdType.MESH,
        )

    for chunk in range(chunks):
        sibling_parts(chunk).start()

    @pl.when(slab < gz_count - 1)
    def _():
        halo_up().start()

    @pl.when(slab > 0)
    def _():
        halo_down().start()

    for chunk in range(chunks):
        sibling_parts(chunk).wait_recv()
        for p in direct:
            sums[chunk][p] = parts[chunk][p] + landed[chunk][half + p]
            reduce_copy(chunk, p).start()
        sums[chunk][0] = parts[chunk][0] + landed[chunk][half]

    ones = jnp.ones((16, rays), jnp.bfloat16)
    for k in range(listed):
        terms[k] = lax.dot_general(
            ones, mats[0, k], (((1,), (1,)), ((), ())), preferred_element_type=jnp.float32
        )[:TILE]
    padded[TILE : TILE + depth, :] = vol[...]

    @pl.when(slab == 0)
    def _():
        padded[:TILE, :] = jnp.zeros((TILE, vxy), jnp.float32)

    @pl.when(slab == gz_count - 1)
    def _():
        padded[TILE + depth :, :] = jnp.zeros((TILE, vxy), jnp.float32)

    def smooth():
        @pl.when(slab > 0)
        def _():
            halo_up().wait_recv()

        @pl.when(slab < gz_count - 1)
        def _():
            halo_down().wait_recv()

        for lane in range(0, vxy, LANES):
            lanes = slice(lane, lane + LANES)
            diffs = padded[TILE : TILE + depth + 1, lanes] - padded[TILE - 1 : TILE + depth, lanes]
            slopes = diffs * lax.rsqrt(diffs * diffs + smooth_sq)
            smoothed[:, lanes] = vol[:, lanes] - tv_weight * (slopes[:depth] - slopes[1:])

    smooth()
    rowsum = None
    for chunk in range(chunks):
        total = sums[chunk][0]
        for p in range(1, half):
            reduce_copy(chunk, p).wait_recv()
            total = total + landed[chunk][p]
        if chunk == 0:
            rowsum = total[rows : rows + 1]
        top = chunk * rows
        ray_values[chunk][0] = (sino[top : top + rows, :] - total[:rows]) / rowsum
        for p in direct:
            gather_copy(chunk, p).start()
        relay_copy(chunk, 0).start()
    for chunk in range(chunks):
        for p in range(1, half):
            gather_copy(chunk, p).wait_recv()
            relay_copy(chunk, p).start()
    for chunk in range(chunks):
        for p in range(half):
            relay_copy(chunk, p).wait_recv()
    for chunk in range(chunks):
        sibling_parts(chunk).wait_send()
        for p in range(half):
            if p:
                reduce_copy(chunk, p).wait_send()
                gather_copy(chunk, p).wait_send()
            relay_copy(chunk, p).wait_send()

    @pl.when(slab < gz_count - 1)
    def _():
        halo_up().wait_send()

    @pl.when(slab > 0)
    def _():
        halo_down().wait_send()


def back_kernel(cfg, smoothed, terms, mats, offsets, lists, owner_map, *refs):
    count, bits, depth, vxy, width, rays, listed, chunks, gz_count = cfg
    rows = depth // chunks
    ray_values = refs[:chunks]
    new_vol, weighted_out, spread = refs[chunks:]
    me = lax.axis_index("xy")
    span = width + LANES
    margin = vxy - span
    high = depth + TILE
    for chunk in range(chunks):
        weighted_out[chunk * rows : (chunk + 1) * rows, :] = ray_values[chunk][0]
    spread[:, :, :margin] = jnp.zeros((listed, high, margin), jnp.float32)
    spread[:, :, margin + span :] = jnp.zeros((listed, high, margin), jnp.float32)
    places = []
    for k in range(listed):
        place = position_of(owner_map[lists[k, me]], me, bits)
        needed = jnp.concatenate([ray_values[c][place] for c in range(chunks)], axis=0)
        stacked = lax.dot_general(
            jnp.concatenate(split_terms(needed, TERMS), axis=0),
            mats[0, k],
            (((1,), (1,)), ((), ())),
            preferred_element_type=jnp.float32,
        )
        start, shift = band(offsets, k, vxy, width)
        piece = jnp.concatenate([sum_slabs(stacked, TERMS, depth), terms[k]], axis=0)
        wide = jnp.concatenate([piece, jnp.zeros((high, LANES), jnp.float32)], axis=1)
        spread[k, :, margin : margin + span] = pltpu.roll(wide, shift, 1)
        places.append(margin - start)
    for lane in range(0, vxy, LANES):
        total = None
        for k in range(listed):
            piece = spread[k, :, pl.ds(pl.multiple_of(places[k] + lane, LANES), LANES)]
            total = piece if total is None else total + piece
        lanes = slice(lane, lane + LANES)
        scale = relax / jnp.maximum(total[depth : depth + 1], 1.0)
        new_vol[:, lanes] = smoothed[:, lanes] + total[:depth] * scale


def per_device(cfg, volume, sinogram, ray_mats, offsets, ray_lists, owner_map):
    count, bits, depth, vxy, width, rays, listed, chunks, gz_count = cfg
    rows = depth // chunks
    high = [rows + (TILE if chunk == 0 else 0) for chunk in range(chunks)]
    f32 = jnp.float32
    vmem = pl.BlockSpec(memory_space=pltpu.VMEM)
    smem = pl.BlockSpec(memory_space=pltpu.SMEM)
    limit = 24 * 1024 * 1024

    def shape(*dims):
        return jax.ShapeDtypeStruct(dims, f32)

    lists = ray_lists.T
    parts = pl.pallas_call(
        functools.partial(project_kernel, cfg),
        out_shape=tuple(shape(count, h, rays) for h in high),
        in_specs=[vmem, vmem, smem, smem, smem],
        out_specs=(vmem,) * chunks,
        scratch_shapes=[pltpu.VMEM((listed + 1, depth + TILE, rays), f32)],
        compiler_params=pltpu.CompilerParams(vmem_limit_bytes=limit),
    )(volume, ray_mats, offsets, lists, owner_map)

    *ray_values, terms, smoothed = pl.pallas_call(
        functools.partial(exchange_kernel, cfg),
        out_shape=tuple(shape(count, rows, rays) for _ in range(chunks))
        + (shape(listed, TILE, width), shape(depth, vxy)),
        in_specs=[vmem] * (3 + chunks),
        out_specs=(vmem,) * (chunks + 2),
        scratch_shapes=[pltpu.VMEM((count // 2, h, rays), f32) for h in high]
        + [pltpu.VMEM((count, h, rays), f32) for h in high]
        + [
            pltpu.VMEM((depth + 2 * TILE, vxy), f32),
            pltpu.SemaphoreType.DMA((chunks, 3 * count // 2)),
            pltpu.SemaphoreType.DMA((chunks, 3 * count // 2)),
            pltpu.SemaphoreType.DMA((2,)),
            pltpu.SemaphoreType.DMA((2,)),
        ],
        compiler_params=pltpu.CompilerParams(
            collective_id=0, has_side_effects=True, vmem_limit_bytes=limit
        ),
    )(volume, sinogram, ray_mats, *parts)

    return pl.pallas_call(
        functools.partial(back_kernel, cfg),
        out_shape=(shape(depth, vxy), shape(depth, rays)),
        in_specs=[vmem] * 3 + [smem] * 3 + [vmem] * chunks,
        out_specs=(vmem, vmem),
        scratch_shapes=[pltpu.VMEM((listed, depth + TILE, 2 * vxy - width - LANES), f32)],
        compiler_params=pltpu.CompilerParams(vmem_limit_bytes=limit),
    )(smoothed, terms, ray_mats, offsets, lists, owner_map, *ray_values)


def solution(mesh):
    in_specs = (P("gz", "xy"), P("gz", "xy"), P("xy", None, None, None), P("xy", None), P(), P())
    out_specs = (P("gz", "xy"), P("gz", "xy"))
    count = mesh.shape["xy"]
    gz_count = mesh.shape["gz"]

    def whole(volume, sinogram, ray_mats, offsets, ray_lists, owner_map):
        cfg = (
            count,
            count.bit_length() - 1,
            volume.shape[0] // gz_count,
            volume.shape[1] // count,
            ray_mats.shape[2],
            ray_mats.shape[3],
            ray_mats.shape[1],
            CHUNKS,
            gz_count,
        )
        return jax.shard_map(
            functools.partial(per_device, cfg),
            mesh=mesh,
            in_specs=in_specs,
            out_specs=out_specs,
            check_vma=False,
        )(volume, sinogram, ray_mats, offsets, ray_lists, owner_map)

    return whole
```

```python
import functools

import jax
import jax.numpy as jnp
from jax import lax
from jax.experimental import pallas as pl
from jax.experimental.pallas import tpu as pltpu
from jax.sharding import PartitionSpec as P

relax = 1.0
tv_weight = 0.2
smooth_sq = 0.01

LANES = 128
TILE = 8
CHUNKS = 2
TERMS = 3


def split_terms(x, terms):
    parts = []
    for _ in range(terms):
        part = x.astype(jnp.bfloat16)
        parts.append(part)
        x = x - part.astype(jnp.float32)
    return parts


def flip(index, bit):
    step = 1 << bit
    return index + step * (1 - 2 * ((index // step) % 2))


def sum_slabs(stacked, terms, rows):
    total = stacked[(terms - 1) * rows : terms * rows]
    for term in range(terms - 2, -1, -1):
        total = total + stacked[term * rows : (term + 1) * rows]
    return total


def partner_at(me, position, bits):
    other = flip(me, 0) if (position >> (bits - 1)) & 1 else me
    for bit in range(1, bits):
        if (position >> (bit - 1)) & 1:
            other = flip(other, bit)
    return other


def position_of(owner, me, bits):
    place = ((owner + me) % 2) * (1 << (bits - 1))
    for bit in range(1, bits):
        step = 1 << bit
        place = place + ((owner // step + me // step) % 2) * (1 << (bit - 1))
    return place


def band(offsets, k, vxy, width):
    last_base = (vxy - width) // LANES - 1
    base = jnp.minimum(offsets[0, k] // LANES, last_base)
    return base * LANES, offsets[0, k] - base * LANES


def project_kernel(cfg, vol, mats, offsets, lists, owner_map, *refs):
    count, bits, depth, vxy, width, rays, listed, chunks, gz_count = cfg
    rows = depth // chunks
    parts = refs[:chunks]
    found = refs[chunks]
    me = lax.axis_index("xy")
    span = width + LANES
    owners = [owner_map[lists[k, me]] for k in range(listed)]
    ones = jnp.ones((16, width), jnp.bfloat16)
    found[listed] = jnp.zeros((depth + TILE, rays), jnp.float32)
    for k in range(listed):
        start, shift = band(offsets, k, vxy, width)
        window = vol[:, pl.ds(pl.multiple_of(start, LANES), span)]
        window = pltpu.roll(window, span - shift, 1)[:, :width]
        lhs = jnp.concatenate(split_terms(window, TERMS) + [ones], axis=0)
        product = jnp.dot(lhs, mats[0, k], preferred_element_type=jnp.float32)
        found[k, :depth] = sum_slabs(product, TERMS, depth)
        found[k, depth:] = product[TERMS * depth : TERMS * depth + TILE]
    for position in range(count):
        owner = partner_at(me, position, bits)
        slot = jnp.int32(listed)
        for k in range(listed):
            slot = jnp.where(owners[k] == owner, jnp.int32(k), slot)
        for chunk in range(chunks):
            top = chunk * rows
            parts[chunk][position, :rows] = found[slot, top : top + rows]
            if chunk == 0:
                parts[chunk][position, rows:] = found[slot, depth:]


def exchange_kernel(cfg, vol, sino, mats, *refs):
    count, bits, depth, vxy, width, rays, listed, chunks, gz_count = cfg
    rows = depth // chunks
    half = count // 2
    refs = list(refs)

    def take(number):
        taken = refs[:number]
        del refs[:number]
        return taken

    parts = take(chunks)
    ray_values = take(chunks)
    terms, smoothed = take(2)
    sums = take(chunks)
    landed = take(chunks)
    padded, send_sem, recv_sem, halo_send, halo_recv = refs

    me = lax.axis_index("xy")
    slab = lax.axis_index("gz")
    sibling = flip(me, 0)
    direct = list(range(half - 1, 0, -1))
    partners = [sibling] + [partner_at(me, p, bits) for p in range(1, half)]

    barrier = pltpu.get_barrier_semaphore()
    for partner in partners:
        pl.semaphore_signal(barrier, inc=1, device_id={"xy": partner}, device_id_type=pl.DeviceIdType.MESH)

    @pl.when(slab > 0)
    def _():
        pl.semaphore_signal(barrier, inc=1, device_id={"gz": slab - 1}, device_id_type=pl.DeviceIdType.MESH)

    @pl.when(slab < gz_count - 1)
    def _():
        pl.semaphore_signal(barrier, inc=1, device_id={"gz": slab + 1}, device_id_type=pl.DeviceIdType.MESH)

    has_below = (slab > 0).astype(jnp.int32)
    has_above = (slab < gz_count - 1).astype(jnp.int32)
    pl.semaphore_wait(barrier, half + has_below + has_above)

    def remote(src, dst, chunk, number, partner):
        return pltpu.make_async_remote_copy(
            src_ref=src,
            dst_ref=dst,
            send_sem=send_sem.at[chunk, number],
            recv_sem=recv_sem.at[chunk, number],
            device_id={"xy": partner},
            device_id_type=pl.DeviceIdType.MESH,
        )

    def sibling_parts(chunk):
        return remote(
            parts[chunk].at[pl.ds(half, half)], landed[chunk].at[pl.ds(half, half)], chunk, 0, sibling
        )

    def reduce_copy(chunk, p):
        return remote(sums[chunk].at[p], landed[chunk].at[p], chunk, p, partners[p])

    def gather_copy(chunk, p):
        return remote(ray_values[chunk].at[0], ray_values[chunk].at[p], chunk, half + p, partners[p])

    def relay_copy(chunk, p):
        return remote(
            ray_values[chunk].at[p], ray_values[chunk].at[half + p], chunk, 2 * half + p, sibling
        )

    def halo_up():
        return pltpu.make_async_remote_copy(
            src_ref=vol.at[pl.ds(depth - TILE, TILE)],
            dst_ref=padded.at[pl.ds(0, TILE)],
            send_sem=halo_send.at[0],
            recv_sem=halo_recv.at[0],
            device_id={"gz": slab + 1},
            device_id_type=pl.DeviceIdType.MESH,
        )

    def halo_down():
        return pltpu.make_async_remote_copy(
            src_ref=vol.at[pl.ds(0, TILE)],
            dst_ref=padded.at[pl.ds(TILE + depth, TILE)],
            send_sem=halo_send.at[1],
            recv_sem=halo_recv.at[1],
            device_id={"gz": slab - 1},
            device_id_type=pl.DeviceIdType.MESH,
        )

    for chunk in range(chunks):
        sibling_parts(chunk).start()

    @pl.when(slab < gz_count - 1)
    def _():
        halo_up().start()

    @pl.when(slab > 0)
    def _():
        halo_down().start()

    for chunk in range(chunks):
        sibling_parts(chunk).wait_recv()
        for p in direct:
            sums[chunk][p] = parts[chunk][p] + landed[chunk][half + p]
            reduce_copy(chunk, p).start()
        sums[chunk][0] = parts[chunk][0] + landed[chunk][half]

    ones = jnp.ones((16, rays), jnp.bfloat16)
    for k in range(listed):
        terms[k] = lax.dot_general(
            ones, mats[0, k], (((1,), (1,)), ((), ())), preferred_element_type=jnp.float32
        )[:TILE]
    padded[TILE : TILE + depth, :] = vol[...]

    @pl.when(slab == 0)
    def _():
        padded[:TILE, :] = jnp.zeros((TILE, vxy), jnp.float32)

    @pl.when(slab == gz_count - 1)
    def _():
        padded[TILE + depth :, :] = jnp.zeros((TILE, vxy), jnp.float32)

    def smooth():
        @pl.when(slab > 0)
        def _():
            halo_up().wait_recv()

        @pl.when(slab < gz_count - 1)
        def _():
            halo_down().wait_recv()

        for lane in range(0, vxy, LANES):
            lanes = slice(lane, lane + LANES)
            diffs = padded[TILE : TILE + depth + 1, lanes] - padded[TILE - 1 : TILE + depth, lanes]
            slopes = diffs * lax.rsqrt(diffs * diffs + smooth_sq)
            smoothed[:, lanes] = vol[:, lanes] - tv_weight * (slopes[:depth] - slopes[1:])

    smooth()
    rowsum = None
    for chunk in range(chunks):
        total = sums[chunk][0]
        for p in range(1, half):
            reduce_copy(chunk, p).wait_recv()
            total = total + landed[chunk][p]
        if chunk == 0:
            rowsum = total[rows : rows + 1]
        top = chunk * rows
        ray_values[chunk][0] = (sino[top : top + rows, :] - total[:rows]) / rowsum
        for p in direct:
            gather_copy(chunk, p).start()
        relay_copy(chunk, 0).start()
    for chunk in range(chunks):
        for p in range(1, half):
            gather_copy(chunk, p).wait_recv()
            relay_copy(chunk, p).start()
    for chunk in range(chunks):
        for p in range(half):
            relay_copy(chunk, p).wait_recv()
    for chunk in range(chunks):
        sibling_parts(chunk).wait_send()
        for p in range(half):
            if p:
                reduce_copy(chunk, p).wait_send()
                gather_copy(chunk, p).wait_send()
            relay_copy(chunk, p).wait_send()

    @pl.when(slab < gz_count - 1)
    def _():
        halo_up().wait_send()

    @pl.when(slab > 0)
    def _():
        halo_down().wait_send()


def back_kernel(cfg, smoothed, terms, mats, offsets, lists, owner_map, *refs):
    count, bits, depth, vxy, width, rays, listed, chunks, gz_count = cfg
    rows = depth // chunks
    ray_values = refs[:chunks]
    new_vol, weighted_out, spread = refs[chunks:]
    me = lax.axis_index("xy")
    span = width + LANES
    margin = vxy - span
    high = depth + TILE
    for chunk in range(chunks):
        weighted_out[chunk * rows : (chunk + 1) * rows, :] = ray_values[chunk][0]
    spread[:, :, :margin] = jnp.zeros((listed, high, margin), jnp.float32)
    spread[:, :, margin + span :] = jnp.zeros((listed, high, margin), jnp.float32)
    places = []
    for k in range(listed):
        place = position_of(owner_map[lists[k, me]], me, bits)
        needed = jnp.concatenate([ray_values[c][place] for c in range(chunks)], axis=0)
        stacked = lax.dot_general(
            jnp.concatenate(split_terms(needed, TERMS), axis=0),
            mats[0, k],
            (((1,), (1,)), ((), ())),
            preferred_element_type=jnp.float32,
        )
        start, shift = band(offsets, k, vxy, width)
        piece = jnp.concatenate([sum_slabs(stacked, TERMS, depth), terms[k]], axis=0)
        wide = jnp.concatenate([piece, jnp.zeros((high, LANES), jnp.float32)], axis=1)
        spread[k, :, margin : margin + span] = pltpu.roll(wide, shift, 1)
        places.append(margin - start)
    for lane in range(0, vxy, LANES):
        total = None
        for k in range(listed):
            piece = spread[k, :, pl.ds(pl.multiple_of(places[k] + lane, LANES), LANES)]
            total = piece if total is None else total + piece
        lanes = slice(lane, lane + LANES)
        scale = relax / jnp.maximum(total[depth : depth + 1], 1.0)
        new_vol[:, lanes] = smoothed[:, lanes] + total[:depth] * scale


def per_device(cfg, volume, sinogram, ray_mats, offsets, ray_lists, owner_map):
    count, bits, depth, vxy, width, rays, listed, chunks, gz_count = cfg
    rows = depth // chunks
    high = [rows + (TILE if chunk == 0 else 0) for chunk in range(chunks)]
    f32 = jnp.float32
    vmem = pl.BlockSpec(memory_space=pltpu.VMEM)
    smem = pl.BlockSpec(memory_space=pltpu.SMEM)
    limit = 24 * 1024 * 1024

    def shape(*dims):
        return jax.ShapeDtypeStruct(dims, f32)

    lists = ray_lists.T
    parts = pl.pallas_call(
        functools.partial(project_kernel, cfg),
        out_shape=tuple(shape(count, h, rays) for h in high),
        in_specs=[vmem, vmem, smem, smem, smem],
        out_specs=(vmem,) * chunks,
        scratch_shapes=[pltpu.VMEM((listed + 1, depth + TILE, rays), f32)],
        compiler_params=pltpu.CompilerParams(vmem_limit_bytes=limit),
    )(volume, ray_mats, offsets, lists, owner_map)

    *ray_values, terms, smoothed = pl.pallas_call(
        functools.partial(exchange_kernel, cfg),
        out_shape=tuple(shape(count, rows, rays) for _ in range(chunks))
        + (shape(listed, TILE, width), shape(depth, vxy)),
        in_specs=[vmem] * (3 + chunks),
        out_specs=(vmem,) * (chunks + 2),
        scratch_shapes=[pltpu.VMEM((count // 2, h, rays), f32) for h in high]
        + [pltpu.VMEM((count, h, rays), f32) for h in high]
        + [
            pltpu.VMEM((depth + 2 * TILE, vxy), f32),
            pltpu.SemaphoreType.DMA((chunks, 3 * count // 2)),
            pltpu.SemaphoreType.DMA((chunks, 3 * count // 2)),
            pltpu.SemaphoreType.DMA((2,)),
            pltpu.SemaphoreType.DMA((2,)),
        ],
        compiler_params=pltpu.CompilerParams(
            collective_id=0, has_side_effects=True, vmem_limit_bytes=limit
        ),
    )(volume, sinogram, ray_mats, *parts)

    return pl.pallas_call(
        functools.partial(back_kernel, cfg),
        out_shape=(shape(depth, vxy), shape(depth, rays)),
        in_specs=[vmem] * 3 + [smem] * 3 + [vmem] * chunks,
        out_specs=(vmem, vmem),
        scratch_shapes=[pltpu.VMEM((listed, depth + TILE, 2 * vxy - width - LANES), f32)],
        compiler_params=pltpu.CompilerParams(vmem_limit_bytes=limit),
    )(smoothed, terms, ray_mats, offsets, lists, owner_map, *ray_values)


def solution(mesh):
    in_specs = (P("gz", "xy"), P("gz", "xy"), P("xy", None, None, None), P("xy", None), P(), P())
    out_specs = (P("gz", "xy"), P("gz", "xy"))
    count = mesh.shape["xy"]
    gz_count = mesh.shape["gz"]

    def whole(volume, sinogram, ray_mats, offsets, ray_lists, owner_map):
        cfg = (
            count,
            count.bit_length() - 1,
            volume.shape[0] // gz_count,
            volume.shape[1] // count,
            ray_mats.shape[2],
            ray_mats.shape[3],
            ray_mats.shape[1],
            CHUNKS,
            gz_count,
        )
        return jax.shard_map(
            functools.partial(per_device, cfg),
            mesh=mesh,
            in_specs=in_specs,
            out_specs=out_specs,
            check_vma=False,
        )(volume, sinogram, ray_mats, offsets, ray_lists, owner_map)

    return whole
```
